32 devices in a mesh: expert: 4 (over z), mp: 8 (over y, x, core).
Axes of the slice: x: 2, y: 2, z: 4, core: 2. Of those that a mesh axis runs over, the one named last changes fastest.
Arguments:
- tokens: bfloat16 [2048, 2048], P('expert', 'mp'), may hold values from -6 to 6
- expert_route: int32 [2048, 2], P('expert'), may hold values from 0 to 3, all different within a row; in each aligned block of 512 rows (0 to 511, 512 to 1023, ...) at most 512 rows name the same one
- route_gate: float32 [2048, 2], P('expert'), may hold values from 0.05 to 1
- request_lengths: int32 [16], replicated, may hold values from 1 to 1024, 2048 in all
- request_adapter: int32 [16], replicated, may hold values from 0 to 63, as said below
- request_order: int32 [16], replicated, may hold values from 0 to 15, each once
- gate_weight: bfloat16 [4, 5632, 2048], P('expert', 'mp'), may hold values from -0.125 to 0.125
- up_weight: bfloat16 [4, 5632, 2048], P('expert', 'mp'), may hold values from -0.125 to 0.125
- down_weight: bfloat16 [4, 5632, 2048], P('expert', 'mp'), may hold values from -0.109375 to 0.109375
- adapter_in: bfloat16 [4, 1024, 2048], P('expert', 'mp'), may hold values from -0.125 to 0.125
- adapter_out: bfloat16 [4, 5632, 1024], P('expert', 'mp'), may hold values from -1.5 to 1.5
Outputs:
- mixed: bfloat16 [2048, 2048], P('expert', 'mp')
The draws below stay inside these ranges and needn't reach their ends.
Inputs may be any that keep to these rules, and one draw needn't show every extreme that they name: `expert_route`: the two entries of a row differ; within each aligned block of 512 rows (the tokens held at one position along `expert`) no expert is named by more than 512 rows, and in some block some expert is named by exactly 512 rows. `request_lengths`: they sum to 2048; the largest is 1024. `request_order`: each request index appears once. `request_adapter`: exactly 16 different adapters appear.
All inputs are finite; a program needn't handle non-finite values.
Results may differ from the reference program's by a relative error of at most 0.035.
Values may be sent and summed in bfloat16 or wider, within the bound.
A program may use at most 64 MiB of HBM per device.

```python
import math
import jax
import jax.numpy as jnp
import numpy as np
from jax import lax

D = 2048
FF = 5632
RANK = 16
ADAPTERS = 64
USED = 16
TOPK = 2
TOK_E = 512
EXPERTS = 4
CAP = 512
TOKENS = 2048
REQS = 16
MOST_LEN = 1024
N_EXPERT = 4
N_MP = 8


def draw_request_adapter(key, part):
    pool_key = jax.random.fold_in(key, 11)
    pick_key = jax.random.fold_in(key, 12)
    order_key = jax.random.fold_in(key, 13)
    middle = jax.random.permutation(pool_key, jnp.arange(1, ADAPTERS - 1, dtype=jnp.int32))[:USED - 2]
    ends_pair = jnp.array([0, ADAPTERS - 1], dtype=jnp.int32)
    adapter_pool = jnp.concatenate([ends_pair, middle.astype(jnp.int32)]).astype(jnp.int32)
    request_ids = jnp.arange(REQS, dtype=jnp.int32)
    assigned = jnp.where(request_ids < USED, request_ids, jax.random.randint(pick_key, (REQS,), 0, USED, dtype=jnp.int32))
    assigned = jax.random.permutation(order_key, assigned)
    return adapter_pool[assigned].astype(jnp.int32)


def raised(drawn, rng, source, target, shards_of, factor):
    def block_of(dim):
        return (jnp.arange(drawn.shape[dim]) // (drawn.shape[dim] // shards_of)).reshape((-1,) + (1,) * (drawn.ndim - 1 - dim))

    one_side = jax.random.permutation(rng, shards_of)[block_of(target)]
    other_side = (block_of(target) + shards_of // 2) % shards_of
    return jnp.where((block_of(source) == one_side) | (block_of(source) == other_side), factor * drawn, drawn)


def block_levels(key, extent, split, smallest, high):
    loudness = 1.0
    for position, blocks in split:
        heights = jax.random.uniform(jax.random.fold_in(jax.random.fold_in(key, 6), position), (blocks,), jnp.float32, smallest / len(split), high / len(split))
        loudness = loudness * jnp.repeat(jnp.exp(heights), extent[position] // blocks).reshape((-1,) + (1,) * (len(extent) - 1 - position))
    return loudness


def split_up(amount, total, reach, skew):
    loads = [(1 << 20) // math.isqrt(rank ** skew) + 1 for rank in range(2, amount + 1)]
    surplus, counts = total - reach - (amount - 1), [1] * (amount - 1)
    while surplus > 0:
        movable = [i for i in range(amount - 1) if counts[i] < reach]
        mass, left = sum([loads[i] for i in movable]), surplus
        for i in movable:
            more = min(reach - counts[i], max(1, left * loads[i] // mass), surplus)
            counts[i] = counts[i] + more
            surplus = surplus - more
    return np.array([reach] + counts)


def uneven(stream_key, amount, total, most, lean):
    if amount == 2:
        one = jax.random.randint(stream_key, (), max(1, total - most), min(most, total - 1) + 1)
        return jnp.stack([one, total - one])
    sizes = jnp.asarray(split_up(amount, total, most, lean), jnp.int32)
    twos = (amount - 1) // 2
    source_of, receiver = sizes[1:1 + 2 * twos:2], sizes[2:2 + 2 * twos:2]
    margin = jnp.minimum(source_of - 1, most - receiver)
    moved = jax.random.randint(jax.random.fold_in(stream_key, 1), (twos,), 0, 1 << 20) % (margin + 1)
    sizes = sizes.at[1:1 + 2 * twos:2].set(source_of - moved).at[2:2 + 2 * twos:2].set(receiver + moved)
    return sizes[jax.random.permutation(jax.random.fold_in(stream_key, 2), amount)]


def deal_out(own_key, own, number, rows, number_of, top, bound, lean):
    ranking = jax.random.permutation(own_key, number_of)
    packed, usual = portions_of(number_of, rows * top, bound, lean, True), portions_of(number_of, rows * top, bound, lean, False)
    places = jnp.arange(number_of)

    def named(sizes, rotation):
        used = int((sizes > 0).sum())
        fixed = max(1, used // 4)
        passed = fixed + (places - fixed + rotation * (used - fixed)) % max(1, number_of - fixed)
        return jnp.zeros((number_of,), jnp.int32).at[ranking[jnp.where(places < fixed, places, passed)]].set(jnp.asarray(sizes, jnp.int32))

    sizes = jnp.where(number % 4 == 0, named(packed, number // 4), named(usual, number - number // 4 - 1))
    mixed = jax.random.permutation(jax.random.fold_in(own, 3), number_of)
    source_of, taker = mixed[0:number_of // 2 * 2:2], mixed[1:number_of // 2 * 2:2]
    slack = jnp.minimum(sizes[source_of] - 1, bound - sizes[taker]) // 2
    slack = jnp.where((source_of == ranking[0]) | (taker == ranking[0]) | (sizes[taker] == 0), 0, jnp.maximum(slack, 0))
    passed = jax.random.randint(jax.random.fold_in(own, 4), (number_of // 2,), 0, 1 << 20) % (slack + 1)
    sizes = sizes.at[source_of].add(-passed).at[taker].add(passed)
    labels = jnp.searchsorted(jnp.cumsum(sizes), jnp.arange(rows * top), side="right").astype(jnp.int32)
    grid = labels.reshape(top, rows).T
    grid = grid[jax.random.permutation(jax.random.fold_in(own, 1), rows)]
    rotation = jax.random.randint(jax.random.fold_in(own, 2), (rows, 1), 0, top)
    return jnp.take_along_axis(grid, (jnp.arange(top)[None, :] + rotation) % top, axis=1)


def portions_of(count, total, bound, lean, full):
    portions = [(1 << 20) // math.isqrt(standing ** lean) + 1 for standing in range(1, count + 1)]
    largest = bound if full else min(bound, max(-(-total // count), total * portions[0] // sum(portions)))
    least = 1 if total - largest >= count - 1 else 0
    given, spare = [largest] + [least] * (count - 1), total - largest - least * (count - 1)
    while spare > 0:
        candidates = [i for i in range(1, count) if given[i] < largest] or [i for i in range(1, count) if given[i] < bound]
        mass, left = sum([portions[i] for i in candidates]), spare
        for i in candidates:
            addition = min(bound - given[i], max(1, left * portions[i] // mass), spare)
            given[i] = given[i] + addition
            spare = spare - addition
    return np.array(given)


def centred(rng, dims, width, most, cuts=(), held_as=jnp.bfloat16):
    values = jax.random.normal(rng, dims, jnp.float32) * width
    if len(cuts) > 0:
        values = block_levels(rng, dims, cuts, -0.22, 0.18) * values
    return jnp.clip(values, min=-most, max=most).astype(held_as)


def heavy_noise(key, extent, scale, reach, shards, heavy, kind=jnp.bfloat16):
    values = scale * jax.random.normal(key, extent, jnp.float32)
    if shards:
        values = values * block_levels(key, extent, shards, -0.22, 0.18)
    return jnp.clip(raised(values, jax.random.fold_in(key, 3), *heavy), -reach, reach).astype(kind)


def setup_inputs(seed: int = 0) -> dict:
    key_of = jax.random.split(jax.random.key(seed), 12)
    tokens = centred(key_of[0], (TOKENS, D), 1.0, 6.0, ((0, 4), (1, 8)))
    expert_route_keys = jax.random.split(jax.random.fold_in(key_of[1], 1), TOKENS // TOK_E)
    expert_route_turns = jax.random.permutation(jax.random.fold_in(key_of[1], 3), TOKENS // TOK_E)
    expert_route = jax.vmap(lambda own, number: deal_out(jax.random.fold_in(key_of[1], 2), own, number, TOK_E, EXPERTS, TOPK, CAP, 2))(expert_route_keys, expert_route_turns).reshape((TOKENS, TOPK))
    route_gate = jnp.clip(0.05 + 0.95 * jax.random.uniform(key_of[2], (TOKENS, TOPK), jnp.float32) ** block_levels(key_of[2], (TOKENS, TOPK), ((0, 4),), -0.2, 0.2), 0.05, 1.0)
    request_lengths = uneven(key_of[3], REQS, TOKENS, MOST_LEN, 2).astype(jnp.int32)
    request_adapter = draw_request_adapter(jax.random.fold_in(key_of[11], 71), 0)
    request_order = jax.random.permutation(key_of[5], REQS).astype(jnp.int32)
    gate_weight = centred(key_of[6], (EXPERTS, FF, D), D ** -0.5, 0.125, ((0, 4), (1, 8)))
    up_weight = centred(key_of[7], (EXPERTS, FF, D), D ** -0.5, 0.125, ((0, 4), (1, 8)))
    down_weight = heavy_noise(key_of[8], (EXPERTS, FF, D), FF ** -0.5, 0.109375, ((0, 4), (1, 8)), (1, 2, 8, 2.0))
    adapter_in = centred(key_of[9], (EXPERTS, ADAPTERS * RANK, D), D ** -0.5, 0.125, ((0, 4), (1, 8)))
    adapter_out = centred(key_of[10], (EXPERTS, FF, ADAPTERS * RANK), RANK ** -0.5, 1.5, ((0, 4), (1, 8)))
    return {"tokens": tokens, "expert_route": expert_route, "route_gate": route_gate, "request_lengths": request_lengths, "request_adapter": request_adapter, "request_order": request_order, "gate_weight": gate_weight, "up_weight": up_weight, "down_weight": down_weight, "adapter_in": adapter_in, "adapter_out": adapter_out}


def token_adapters(request_lengths, request_adapter, request_order, first_token, token_count):
    request_ids = jnp.arange(request_lengths.shape[0], dtype=jnp.int32)
    chosen = (request_order[:, None] == request_ids[None, :]).astype(jnp.int32)
    packed_lengths = jnp.sum(chosen * request_lengths[None, :], axis=1, dtype=jnp.int32)
    packed_adapters = jnp.sum(chosen * request_adapter[None, :], axis=1, dtype=jnp.int32)
    boundary = jnp.cumsum(packed_lengths, dtype=jnp.int32)
    positions = first_token + jnp.arange(token_count, dtype=jnp.int32)
    packed_index = jnp.sum((boundary[None, :] <= positions[:, None]).astype(jnp.int32), axis=1, dtype=jnp.int32)
    matches = (packed_index[:, None] == request_ids[None, :]).astype(jnp.int32)
    return jnp.sum(matches * packed_adapters[None, :], axis=1, dtype=jnp.int32)


def expert_slots(routes, groups, capacity):
    flat_routes = routes.reshape(-1)
    one_hot = (flat_routes[:, None] == jnp.arange(groups, dtype=jnp.int32)[None, :]).astype(jnp.int32)
    before = jnp.cumsum(one_hot, axis=0, dtype=jnp.int32) - one_hot
    seat_index = jnp.sum(before * one_hot, axis=1, dtype=jnp.int32)
    return (flat_routes * capacity + seat_index).reshape(routes.shape)


def contract_last(left, right):
    return lax.dot_general(left, right, (((1,), (1,)), ((), ())), preferred_element_type=jnp.float32)


def expert_block(operands):
    arrived, arrived_adapter, gate_w, up_w, down_w, rank_in, rank_out = operands
    row_count = arrived.shape[0]
    gate_pre = contract_last(arrived, gate_w)
    up_base = contract_last(arrived, up_w)
    rank_all = contract_last(arrived, rank_in)
    chosen = (arrived_adapter[:, None] == jnp.arange(ADAPTERS, dtype=jnp.int32)[None, :]).astype(jnp.float32)
    rank = jnp.sum(rank_all.reshape(row_count, ADAPTERS, RANK) * chosen[:, :, None], axis=1).astype(jnp.bfloat16)
    expanded = (rank[:, None, :] * chosen[:, :, None].astype(jnp.bfloat16)).reshape(row_count, ADAPTERS * RANK)
    up = up_base + contract_last(expanded, rank_out)
    hidden = (jax.nn.silu(gate_pre) * up).astype(jnp.bfloat16)
    block_width = FF // N_MP
    hidden_blocks = jnp.transpose(hidden.reshape(row_count, N_MP, block_width), (1, 0, 2))
    down_blocks = down_w.reshape(N_MP, block_width, D)

    def add_block(totals, pair):
        term = jnp.dot(pair[0], pair[1], preferred_element_type=jnp.float32)
        rounded = lax.optimization_barrier(term.astype(jnp.bfloat16))
        return totals + rounded.astype(jnp.float32), None

    summed, unused = lax.scan(add_block, jnp.zeros((row_count, D), jnp.float32), (hidden_blocks, down_blocks))
    return summed.astype(jnp.bfloat16)


def reference(tokens, expert_route, route_gate, request_lengths, request_adapter, request_order, gate_weight, up_weight, down_weight, adapter_in, adapter_out):
    adapter_of = token_adapters(request_lengths, request_adapter, request_order, 0, TOKENS)
    route_blocks = expert_route.reshape(N_EXPERT, TOK_E, TOPK)
    slots = jax.vmap(lambda block_routes: expert_slots(block_routes, EXPERTS, CAP))(route_blocks)
    seat_index = slots - route_blocks * CAP
    block_ids = jnp.arange(N_EXPERT, dtype=jnp.int32)[:, None, None]
    group_rows = N_EXPERT * CAP
    destination = (route_blocks * group_rows + block_ids * CAP + seat_index).reshape(TOKENS * TOPK)
    token_index = jnp.broadcast_to(jnp.arange(TOKENS, dtype=jnp.int32)[:, None], (TOKENS, TOPK)).reshape(TOKENS * TOPK)
    total_rows = EXPERTS * group_rows
    buffer = jnp.zeros((total_rows, D), jnp.bfloat16).at[destination].set(tokens[token_index])
    buffer_adapter = jnp.full((total_rows,), -1, jnp.int32).at[destination].set(adapter_of[token_index])
    outputs = lax.map(expert_block, (buffer.reshape(EXPERTS, group_rows, D), buffer_adapter.reshape(EXPERTS, group_rows), gate_weight, up_weight, down_weight, adapter_in, adapter_out))
    picked = outputs.reshape(total_rows, D)[destination].astype(jnp.float32).reshape(TOKENS, TOPK, D)
    mixed = jnp.sum(route_gate[:, :, None] * picked, axis=1)
    return mixed.astype(jnp.bfloat16)
```

```python
import functools

import jax
import jax.numpy as jnp
from jax import lax
from jax.experimental import pallas as pl
from jax.experimental.pallas import tpu as pltpu
from jax.sharding import PartitionSpec as P

RANK = 16
ADAPTERS = 64
MESH = pl.DeviceIdType.MESH


def contract_last(left, right):
    return lax.dot_general(
        left, right, (((1,), (1,)), ((), ())), preferred_element_type=jnp.float32
    )


def token_adapters(request_lengths, request_adapter, request_order, token_count):
    request_ids = jnp.arange(request_lengths.shape[0], dtype=jnp.int32)
    chosen = (request_order[:, None] == request_ids[None, :]).astype(jnp.int32)
    packed_lengths = jnp.sum(chosen * request_lengths[None, :], axis=1, dtype=jnp.int32)
    packed_adapters = jnp.sum(chosen * request_adapter[None, :], axis=1, dtype=jnp.int32)
    boundary = jnp.cumsum(packed_lengths, dtype=jnp.int32)
    positions = jnp.arange(token_count, dtype=jnp.int32)
    packed_index = jnp.sum(
        (boundary[None, :] <= positions[:, None]).astype(jnp.int32), axis=1, dtype=jnp.int32
    )
    matches = (packed_index[:, None] == request_ids[None, :]).astype(jnp.int32)
    return jnp.sum(matches * packed_adapters[None, :], axis=1, dtype=jnp.int32)


def plain(
    tokens,
    expert_route,
    route_gate,
    request_lengths,
    request_adapter,
    request_order,
    gate_weight,
    up_weight,
    down_weight,
    adapter_in,
    adapter_out,
):
    groups = lax.axis_size("expert")
    tok_rows, cols = tokens.shape
    own_rows = lax.all_gather(tokens, "expert", axis=0, tiled=True)
    rows = lax.all_gather(own_rows, "mp", axis=1, tiled=True)
    row_count = rows.shape[0]
    adapter_of = token_adapters(request_lengths, request_adapter, request_order, row_count)
    rank_w = adapter_in[0]
    rank_cols = contract_last(rows, rank_w)
    per_device = rank_w.shape[0] // RANK
    local_adapter = adapter_of - lax.axis_index("mp") * per_device
    local_pick = (
        local_adapter[:, None] == jnp.arange(per_device, dtype=jnp.int32)[None, :]
    ).astype(jnp.float32)
    rank_part = jnp.sum(
        rank_cols.reshape(row_count, per_device, RANK) * local_pick[:, :, None], axis=1
    )
    rank = lax.psum(rank_part.astype(jnp.bfloat16), "mp")
    gate_pre = contract_last(rows, gate_weight[0])
    up_base = contract_last(rows, up_weight[0])
    chosen = (adapter_of[:, None] == jnp.arange(ADAPTERS, dtype=jnp.int32)[None, :]).astype(
        jnp.bfloat16
    )
    expanded = (rank[:, None, :] * chosen[:, :, None]).reshape(row_count, ADAPTERS * RANK)
    up = up_base + contract_last(expanded, adapter_out[0])
    hidden = (jax.nn.silu(gate_pre) * up).astype(jnp.bfloat16)
    partial = jnp.dot(hidden, down_weight[0], preferred_element_type=jnp.float32)
    mine = lax.psum_scatter(
        partial.astype(jnp.bfloat16), "mp", scatter_dimension=1, tiled=True
    )
    back = lax.all_to_all(
        mine.reshape(groups, tok_rows, cols), "expert", split_axis=0, concat_axis=0, tiled=True
    )
    expert_ids = jnp.arange(groups, dtype=jnp.int32)
    weights = jnp.sum(
        jnp.where(expert_route[:, :, None] == expert_ids, route_gate[:, :, None], 0.0), axis=1
    )
    mixed = jnp.sum(weights.T[:, :, None] * back.astype(jnp.float32), axis=0)
    return mixed.astype(jnp.bfloat16)


def xor4(a, b):
    return (a + b) % 2 + 2 * ((a // 2 + b // 2) % 2)


def kernel(
    len_ref,
    req_adapter_ref,
    order_ref,
    tok_ref,
    route_ref,
    weigh_ref,
    gw_hbm,
    uw_hbm,
    dw_hbm,
    ain_hbm,
    aout_hbm,
    out_ref,
    gw,
    uw,
    dw,
    ain,
    aout,
    x_buf,
    part,
    pair_in,
    pair_sum,
    quad_in,
    e_buf,
    back,
    rk_buf,
    adp,
    g_ref,
    exp_ref,
    h_ref,
    w_sem,
    loc_sem,
    z_send,
    z_recv,
    xy_send,
    xy_recv,
    dg_send,
    dg_recv,
    sib_send,
    sib_recv,
    rk_send,
    rk_recv,
    r1_send,
    r1_recv,
    r2_send,
    r2_recv,
    e_send,
    e_recv,
):
    T, C = tok_ref.shape
    H = T // 2
    z = lax.axis_index("expert")
    m = lax.axis_index("mp")
    q = m // 2
    c = m % 2
    sibling = (z, 2 * q + 1 - c)

    def chip(j):
        return xor4(q, j)

    def col(index):
        return pl.ds(pl.multiple_of(index * C, C), C)

    def remote(src, dst, send, recv, target):
        return pltpu.make_async_remote_copy(
            src_ref=src, dst_ref=dst, send_sem=send, recv_sem=recv,
            device_id=target, device_id_type=MESH,
        )

    def z_copy(s):
        return remote(
            x_buf.at[0, :, col(m)], x_buf.at[s, :, col(m)],
            z_send.at[s], z_recv.at[s], (xor4(z, s), m),
        )

    def xy_copy(s, j):
        ref = x_buf.at[s, :, col(m)]
        return remote(ref, ref, xy_send.at[s, j], xy_recv.at[s, j], (z, 2 * chip(j) + c))

    def dg_copy(s, j):
        ref = x_buf.at[s, pl.ds(H * (j - 1), H), col(2 * chip(j) + c)]
        return remote(
            ref, ref, dg_send.at[s, j], dg_recv.at[s, j], (z, 2 * chip(3 - j) + c)
        )

    def sib_copy(s, j):
        ref = x_buf.at[s, :, col(2 * chip(j) + c)]
        return remote(ref, ref, sib_send.at[s, j], sib_recv.at[s, j], sibling)

    def rk_copy(s, d):
        return remote(
            rk_buf.at[s, 0], rk_buf.at[s, d],
            rk_send.at[s, d], rk_recv.at[s, d], (z, (m + d) % 8),
        )

    def r1_copy(s, j):
        return remote(
            part.at[s, :, col(2 * j + 1 - c)], pair_in.at[s, :, pl.ds(j * C, C)],
            r1_send.at[s, j], r1_recv.at[s, j], sibling,
        )

    def r2_copy(s, j):
        return remote(
            pair_sum.at[s, :, col(chip(j))], quad_in.at[s, j],
            r2_send.at[s, j], r2_recv.at[s, j], (z, 2 * chip(j) + c),
        )

    def e_copy(s):
        return remote(e_buf.at[s], back.at[s], e_send.at[s], e_recv.at[s], (xor4(z, s), m))

    first = pltpu.make_async_copy(tok_ref, x_buf.at[0, :, col(m)], loc_sem)
    first.start()
    weights = [
        pltpu.make_async_copy(src.at[0], dst, w_sem.at[i])
        for i, (src, dst) in enumerate(
            ((ain_hbm, ain), (gw_hbm, gw), (uw_hbm, uw), (aout_hbm, aout), (dw_hbm, dw))
        )
    ]
    for copy in weights:
        copy.start()

    barrier = pltpu.get_barrier_semaphore()
    for s in range(1, 4):
        pl.semaphore_signal(barrier, inc=1, device_id=(xor4(z, s), m), device_id_type=MESH)
    for d in range(1, 8):
        pl.semaphore_signal(barrier, inc=1, device_id=(z, (m + d) % 8), device_id_type=MESH)
    pl.semaphore_wait(barrier, 10)

    first.wait()

    def begin(s):
        for j in (1, 2):
            xy_copy(s, j).start()
        sib_copy(s, 0).start()

    def forward(s):
        for j in (1, 2):
            xy_copy(s, j).wait_recv()
            dg_copy(s, j).start()
            sib_copy(s, j).start()

    def finish(s):
        for j in (1, 2):
            dg_copy(s, j).wait_recv()
        sib_copy(s, 3).start()
        for j in range(4):
            sib_copy(s, j).wait_recv()

    z_copy(1).start()
    begin(0)
    z_copy(2).start()
    z_copy(3).start()

    start = jnp.int32(0)
    starts, ids = [], []
    for j in range(len_ref.shape[0]):
        request = order_ref[j]
        starts.append(start)
        ids.append(req_adapter_ref[request])
        start = start + len_ref[request]
    for s in range(4):
        position = xor4(z, s) * T + lax.broadcasted_iota(jnp.int32, (1, T), 1)
        value = jnp.zeros((1, T), jnp.int32)
        for at, adapter in zip(starts, ids):
            value = jnp.where(position >= at, adapter, value)
        adp[s] = value

    forward(0)
    for copy in weights:
        copy.wait()

    def quad_finish(s):
        for j in range(1, 4):
            r2_copy(s, j).wait_recv()
        total = pair_sum[s, :, col(q)].astype(jnp.float32)
        for j in range(1, 4):
            total = total + quad_in[s, j].astype(jnp.float32)
        e_buf[s] = total.astype(jnp.bfloat16)

    per_device = ain.shape[0] // RANK

    def step(s, carry):
        @pl.when(s < 3)
        def _():
            z_copy(s + 1).wait_recv()
            begin(s + 1)

        finish(s)
        adapter_row = adp[s]
        rank_cols = contract_last(ain[...], x_buf[s])
        group = lax.broadcasted_iota(jnp.int32, rank_cols.shape, 0) // RANK + per_device * m
        picked = jnp.where(group == adapter_row, rank_cols, 0.0)
        total = picked[0:RANK]
        for g in range(1, per_device):
            total = total + picked[g * RANK : (g + 1) * RANK]
        rk_buf[s, 0] = total.astype(jnp.bfloat16)
        for d in range(1, 8):
            rk_copy(s, d).start()

        g_ref[...] = contract_last(x_buf[s], gw[...])

        @pl.when(s < 3)
        def _():
            forward(s + 1)

        up_base = contract_last(x_buf[s], uw[...])
        for d in range(1, 8):
            rk_copy(s, d).wait_recv()
        rank = rk_buf[s, 0].astype(jnp.float32)
        for d in range(1, 8):
            rank = rank + rk_buf[s, d].astype(jnp.float32)
        rank_cols8 = jnp.concatenate([rank] * 8, axis=0).T
        adapter_cols = jnp.broadcast_to(adapter_row.astype(jnp.float32), (128, T)).T
        lane_group = (lax.broadcasted_iota(jnp.int32, (T, 128), 1) // RANK).astype(jnp.float32)
        for g in range(ADAPTERS // 8):
            exp_ref[:, g * 128 : (g + 1) * 128] = jnp.where(
                lane_group + 8.0 * g == adapter_cols, rank_cols8, 0.0
            ).astype(jnp.bfloat16)
        up = up_base + contract_last(exp_ref[...], aout[...])
        gate = g_ref[...]
        h_ref[...] = (jax.nn.silu(gate) * up).astype(jnp.bfloat16)
        width = 2 * C
        for j in range(4):
            part[s, :, j * width : (j + 1) * width] = jnp.dot(
                h_ref[...], dw[:, j * width : (j + 1) * width],
                preferred_element_type=jnp.float32,
            ).astype(jnp.bfloat16)
            r1_copy(s, j).start()

        @pl.when(s > 0)
        def _():
            quad_finish(s - 1)

        @pl.when(s > 1)
        def _():
            e_copy(s - 1).start()

        for j in range(4):
            r1_copy(s, j).wait_recv()
            pair_sum[s, :, j * C : (j + 1) * C] = (
                part[s, :, col(2 * j + c)].astype(jnp.float32)
                + pair_in[s, :, j * C : (j + 1) * C].astype(jnp.float32)
            ).astype(jnp.bfloat16)
        for j in (3, 1, 2):
            r2_copy(s, j).start()
        return carry

    lax.fori_loop(0, 4, step, 0)
    quad_finish(3)
    e_copy(3).start()

    def weight_of(s):
        hit = route_ref[...] == xor4(z, s)
        return jnp.sum(jnp.where(hit, weigh_ref[...], 0.0), axis=1, keepdims=True)

    mixed = weight_of(0) * e_buf[0].astype(jnp.float32)
    for s in range(1, 4):
        e_copy(s).wait_recv()
        mixed = mixed + weight_of(s) * back[s].astype(jnp.float32)
    out_ref[...] = mixed.astype(jnp.bfloat16)

    for s in range(1, 4):
        z_copy(s).wait_send()
        e_copy(s).wait_send()

    def drain(s, carry):
        for j in (1, 2):
            xy_copy(s, j).wait_send()
            dg_copy(s, j).wait_send()
        for j in range(4):
            sib_copy(s, j).wait_send()
            r1_copy(s, j).wait_send()
        for j in range(1, 4):
            r2_copy(s, j).wait_send()
        for d in range(1, 8):
            rk_copy(s, d).wait_send()
        return carry

    lax.fori_loop(0, 4, drain, 0)


def fused(
    tokens,
    expert_route,
    route_gate,
    request_lengths,
    request_adapter,
    request_order,
    gate_weight,
    up_weight,
    down_weight,
    adapter_in,
    adapter_out,
):
    T, C = tokens.shape
    D = gate_weight.shape[2]
    F = gate_weight.shape[1]
    A = adapter_in.shape[1]
    bf16 = jnp.bfloat16
    dma = pltpu.SemaphoreType.DMA
    vmem = pl.BlockSpec(memory_space=pltpu.VMEM)
    smem = pl.BlockSpec(memory_space=pltpu.SMEM)
    hbm = pl.BlockSpec(memory_space=pl.ANY)
    return pl.pallas_call(
        kernel,
        out_shape=jax.ShapeDtypeStruct((T, C), bf16),
        in_specs=[smem, smem, smem, hbm, vmem, vmem, hbm, hbm, hbm, hbm, hbm],
        out_specs=vmem,
        scratch_shapes=[
            pltpu.VMEM((F, D), bf16),
            pltpu.VMEM((F, D), bf16),
            pltpu.VMEM((F, D), bf16),
            pltpu.VMEM((A, D), bf16),
            pltpu.VMEM((F, ADAPTERS * RANK), bf16),
            pltpu.VMEM((4, T, D), bf16),
            pltpu.VMEM((4, T, D), bf16),
            pltpu.VMEM((4, T, 4 * C), bf16),
            pltpu.VMEM((4, T, 4 * C), bf16),
            pltpu.VMEM((4, 4, T, C), bf16),
            pltpu.VMEM((4, T, C), bf16),
            pltpu.VMEM((4, T, C), bf16),
            pltpu.VMEM((4, 8, RANK, T), bf16),
            pltpu.VMEM((4, 1, T), jnp.int32),
            pltpu.VMEM((T, F), jnp.float32),
            pltpu.VMEM((T, ADAPTERS * RANK), bf16),
            pltpu.VMEM((T, F), bf16),
            dma((5,)),
            dma,
            dma((4,)),
            dma((4,)),
            dma((4, 4)),
            dma((4, 4)),
            dma((4, 4)),
            dma((4, 4)),
            dma((4, 4)),
            dma((4, 4)),
            dma((4, 8)),
            dma((4, 8)),
            dma((4, 4)),
            dma((4, 4)),
            dma((4, 4)),
            dma((4, 4)),
            dma((4,)),
            dma((4,)),
        ],
        compiler_params=pltpu.CompilerParams(
            collective_id=0, has_side_effects=True, vmem_limit_bytes=60 * 1024 * 1024
        ),
        cost_estimate=pl.CostEstimate(
            flops=8 * T * (3 * F * D + A * D + F * ADAPTERS * RANK),
            bytes_accessed=2 * (3 * F * D + A * D + F * ADAPTERS * RANK),
            transcendentals=4 * T * F,
        ),
    )(
        request_lengths,
        request_adapter,
        request_order,
        tokens,
        expert_route,
        route_gate,
        gate_weight,
        up_weight,
        down_weight,
        adapter_in,
        adapter_out,
    )


def solution(mesh):
    in_specs = (
        P("expert", "mp"),
        P("expert", None),
        P("expert", None),
        P(),
        P(),
        P(),
        P("expert", "mp", None),
        P("expert", "mp", None),
        P("expert", "mp", None),
        P("expert", "mp", None),
        P("expert", "mp", None),
    )
    out_specs = P("expert", "mp")
    small = mesh.shape["expert"] == 4 and mesh.shape["mp"] == 8
    return jax.shard_map(
        fused if small else plain,
        mesh=mesh, in_specs=in_specs, out_specs=out_specs, check_vma=False,
    )
```

```python
import functools

import jax
import jax.numpy as jnp
from jax import lax
from jax.experimental import pallas as pl
from jax.experimental.pallas import tpu as pltpu
from jax.sharding import PartitionSpec as P

RANK = 16
ADAPTERS = 64
MESH = pl.DeviceIdType.MESH


def contract_last(left, right):
    return lax.dot_general(
        left, right, (((1,), (1,)), ((), ())), preferred_element_type=jnp.float32
    )


def token_adapters(request_lengths, request_adapter, request_order, token_count):
    request_ids = jnp.arange(request_lengths.shape[0], dtype=jnp.int32)
    chosen = (request_order[:, None] == request_ids[None, :]).astype(jnp.int32)
    packed_lengths = jnp.sum(chosen * request_lengths[None, :], axis=1, dtype=jnp.int32)
    packed_adapters = jnp.sum(chosen * request_adapter[None, :], axis=1, dtype=jnp.int32)
    boundary = jnp.cumsum(packed_lengths, dtype=jnp.int32)
    positions = jnp.arange(token_count, dtype=jnp.int32)
    packed_index = jnp.sum(
        (boundary[None, :] <= positions[:, None]).astype(jnp.int32), axis=1, dtype=jnp.int32
    )
    matches = (packed_index[:, None] == request_ids[None, :]).astype(jnp.int32)
    return jnp.sum(matches * packed_adapters[None, :], axis=1, dtype=jnp.int32)


def plain(
    tokens,
    expert_route,
    route_gate,
    request_lengths,
    request_adapter,
    request_order,
    gate_weight,
    up_weight,
    down_weight,
    adapter_in,
    adapter_out,
):
    groups = lax.axis_size("expert")
    tok_rows, cols = tokens.shape
    own_rows = lax.all_gather(tokens, "expert", axis=0, tiled=True)
    rows = lax.all_gather(own_rows, "mp", axis=1, tiled=True)
    row_count = rows.shape[0]
    adapter_of = token_adapters(request_lengths, request_adapter, request_order, row_count)
    rank_w = adapter_in[0]
    rank_cols = contract_last(rows, rank_w)
    per_device = rank_w.shape[0] // RANK
    local_adapter = adapter_of - lax.axis_index("mp") * per_device
    local_pick = (
        local_adapter[:, None] == jnp.arange(per_device, dtype=jnp.int32)[None, :]
    ).astype(jnp.float32)
    rank_part = jnp.sum(
        rank_cols.reshape(row_count, per_device, RANK) * local_pick[:, :, None], axis=1
    )
    rank = lax.psum(rank_part.astype(jnp.bfloat16), "mp")
    gate_pre = contract_last(rows, gate_weight[0])
    up_base = contract_last(rows, up_weight[0])
    chosen = (adapter_of[:, None] == jnp.arange(ADAPTERS, dtype=jnp.int32)[None, :]).astype(
        jnp.bfloat16
    )
    expanded = (rank[:, None, :] * chosen[:, :, None]).reshape(row_count, ADAPTERS * RANK)
    up = up_base + contract_last(expanded, adapter_out[0])
    hidden = (jax.nn.silu(gate_pre) * up).astype(jnp.bfloat16)
    partial = jnp.dot(hidden, down_weight[0], preferred_element_type=jnp.float32)
    mine = lax.psum_scatter(
        partial.astype(jnp.bfloat16), "mp", scatter_dimension=1, tiled=True
    )
    back = lax.all_to_all(
        mine.reshape(groups, tok_rows, cols), "expert", split_axis=0, concat_axis=0, tiled=True
    )
    expert_ids = jnp.arange(groups, dtype=jnp.int32)
    weights = jnp.sum(
        jnp.where(expert_route[:, :, None] == expert_ids, route_gate[:, :, None], 0.0), axis=1
    )
    mixed = jnp.sum(weights.T[:, :, None] * back.astype(jnp.float32), axis=0)
    return mixed.astype(jnp.bfloat16)


def xor4(a, b):
    return (a + b) % 2 + 2 * ((a // 2 + b // 2) % 2)


def mask_of(s):
    return s // 2 + 2 * (((s + 1) // 2) % 2)


def kernel(
    len_ref,
    req_adapter_ref,
    order_ref,
    tok_ref,
    route_ref,
    weigh_ref,
    gw_hbm,
    uw_hbm,
    dw_hbm,
    ain_hbm,
    aout_hbm,
    out_ref,
    gw,
    uw,
    dw,
    ain,
    aout,
    x_buf,
    part,
    pair_in,
    pair_sum,
    quad_in,
    e_buf,
    back,
    rk_buf,
    adp,
    g_ref,
    exp_ref,
    h_ref,
    w_cols,
    w_sem,
    loc_sem,
    z_send,
    z_recv,
    xy_send,
    xy_recv,
    dg_send,
    dg_recv,
    sib_send,
    sib_recv,
    rk_send,
    rk_recv,
    r1_send,
    r1_recv,
    r2_send,
    r2_recv,
    n_send,
    n_recv,
    e_send,
    e_recv,
):
    T, C = tok_ref.shape
    H = T // 2
    z = lax.axis_index("expert")
    m = lax.axis_index("mp")
    q = m // 2
    c = m % 2
    sibling = (z, 2 * q + 1 - c)

    def chip(j):
        return xor4(q, j)

    def col(index):
        return pl.ds(pl.multiple_of(index * C, C), C)

    def remote(src, dst, send, recv, target):
        return pltpu.make_async_remote_copy(
            src_ref=src, dst_ref=dst, send_sem=send, recv_sem=recv,
            device_id=target, device_id_type=MESH,
        )

    def z_copy(s):
        return remote(
            x_buf.at[0, :, col(m)], x_buf.at[s, :, col(m)],
            z_send.at[s], z_recv.at[s], (xor4(z, mask_of(s)), m),
        )

    def xy_copy(s, j):
        ref = x_buf.at[s, :, col(m)]
        return remote(ref, ref, xy_send.at[s, j], xy_recv.at[s, j], (z, 2 * chip(j) + c))

    def dg_copy(s, j):
        ref = x_buf.at[s, pl.ds(H * (j - 1), H), col(2 * chip(j) + c)]
        return remote(
            ref, ref, dg_send.at[s, j], dg_recv.at[s, j], (z, 2 * chip(3 - j) + c)
        )

    def sib_copy(s, j):
        ref = x_buf.at[s, :, col(2 * chip(j) + c)]
        return remote(ref, ref, sib_send.at[s, j], sib_recv.at[s, j], sibling)

    def rk_copy(s, d):
        return remote(
            rk_buf.at[s, 0], rk_buf.at[s, d],
            rk_send.at[s, d], rk_recv.at[s, d], (z, (m + d) % 8),
        )

    def r1_copy(s, j):
        return remote(
            part.at[s, :, col(2 * chip(j) + 1 - c)], pair_in.at[s, :, col(chip(j))],
            r1_send.at[s, j], r1_recv.at[s, j], sibling,
        )

    def half(h):
        return pl.ds(H * h, H)

    def d_copy(s, j):
        return remote(
            pair_sum.at[s, half(j - 1), col(chip(3))], quad_in.at[s, 3, half(j - 1)],
            r2_send.at[s, j], r2_recv.at[s, j], (z, 2 * chip(j) + c),
        )

    def n_copy(s, j, h):
        i = 2 * (j - 1) + h
        return remote(
            pair_sum.at[s, half(h), col(chip(j))], quad_in.at[s, j, half(h)],
            n_send.at[s, i], n_recv.at[s, i], (z, 2 * chip(j) + c),
        )

    def e_copy(s):
        return remote(e_buf.at[s], back.at[s], e_send.at[s], e_recv.at[s], (xor4(z, mask_of(s)), m))

    first = pltpu.make_async_copy(tok_ref, x_buf.at[0, :, col(m)], loc_sem)
    first.start()
    weights = [
        pltpu.make_async_copy(src.at[0], dst, w_sem.at[i])
        for i, (src, dst) in enumerate(
            ((ain_hbm, ain), (gw_hbm, gw), (uw_hbm, uw), (aout_hbm, aout), (dw_hbm, dw))
        )
    ]
    for copy in weights:
        copy.start()

    barrier = pltpu.get_barrier_semaphore()
    for s in range(1, 4):
        pl.semaphore_signal(barrier, inc=1, device_id=(xor4(z, mask_of(s)), m), device_id_type=MESH)
    for d in range(1, 8):
        pl.semaphore_signal(barrier, inc=1, device_id=(z, (m + d) % 8), device_id_type=MESH)
    pl.semaphore_wait(barrier, 10)

    first.wait()

    def begin(s):
        for j in (1, 2):
            xy_copy(s, j).start()
        sib_copy(s, 0).start()

    def forward(s):
        for j in (1, 2):
            xy_copy(s, j).wait_recv()
            dg_copy(s, j).start()
            sib_copy(s, j).start()

    def finish(s):
        for j in (1, 2):
            dg_copy(s, j).wait_recv()
        sib_copy(s, 3).start()
        for j in range(4):
            sib_copy(s, j).wait_recv()

    z_copy(1).start()
    begin(0)

    start = jnp.int32(0)
    starts, ids = [], []
    for j in range(len_ref.shape[0]):
        request = order_ref[j]
        starts.append(start)
        ids.append(req_adapter_ref[request])
        start = start + len_ref[request]
    for s in range(4):
        position = xor4(z, mask_of(s)) * T + lax.broadcasted_iota(jnp.int32, (1, T), 1)
        value = jnp.zeros((1, T), jnp.int32)
        for at, adapter in zip(starts, ids):
            value = jnp.where(position >= at, adapter, value)
        adp[s] = value

    hits = [
        jnp.sum(
            jnp.where(route_ref[...] == xor4(z, mask_of(s)), weigh_ref[...], 0.0),
            axis=0, keepdims=True,
        )
        for s in range(4)
    ]
    w_cols[...] = jnp.concatenate(hits + [jnp.zeros((124, T), jnp.float32)], axis=0).T

    forward(0)
    z_copy(2).start()
    z_copy(3).start()
    for copy in weights:
        copy.wait()

    def quad_middle(s):
        for j in (1, 2):
            h = j - 1
            d_copy(s, j).wait_recv()
            where = col(chip(3 - j))
            pair_sum[s, half(h), where] = (
                pair_sum[s, half(h), where].astype(jnp.float32)
                + quad_in[s, 3, half(h)].astype(jnp.float32)
            ).astype(jnp.bfloat16)
            n_copy(s, 3 - j, h).start()

    def quad_finish(s):
        for j in (1, 2):
            for h in range(2):
                n_copy(s, j, h).wait_recv()
        e_buf[s] = (
            pair_sum[s, :, col(q)].astype(jnp.float32)
            + quad_in[s, 1].astype(jnp.float32)
            + quad_in[s, 2].astype(jnp.float32)
        ).astype(jnp.bfloat16)

    per_device = ain.shape[0] // RANK

    def step(s, carry):
        @pl.when(s < 3)
        def _():
            z_copy(s + 1).wait_recv()
            begin(s + 1)

        finish(s)
        adapter_row = adp[s]
        rank_cols = contract_last(ain[...], x_buf[s])
        group = lax.broadcasted_iota(jnp.int32, rank_cols.shape, 0) // RANK + per_device * m
        picked = jnp.where(group == adapter_row, rank_cols, 0.0)
        total = picked[0:RANK]
        for g in range(1, per_device):
            total = total + picked[g * RANK : (g + 1) * RANK]
        rk_buf[s, 0] = total.astype(jnp.bfloat16)
        for d in range(1, 8):
            rk_copy(s, d).start()

        g_ref[...] = contract_last(x_buf[s], gw[...])

        @pl.when(s > 0)
        def _():
            quad_middle(s - 1)

        @pl.when(s < 3)
        def _():
            forward(s + 1)

        up_base = contract_last(x_buf[s], uw[...])
        for d in range(1, 8):
            rk_copy(s, d).wait_recv()
        rank = rk_buf[s, 0].astype(jnp.float32)
        for d in range(1, 8):
            rank = rank + rk_buf[s, d].astype(jnp.float32)
        rank_cols8 = jnp.concatenate([rank] * 8, axis=0).T
        adapter_cols = jnp.broadcast_to(adapter_row.astype(jnp.float32), (128, T)).T
        lane_group = (lax.broadcasted_iota(jnp.int32, (T, 128), 1) // RANK).astype(jnp.float32)
        for g in range(ADAPTERS // 8):
            exp_ref[:, g * 128 : (g + 1) * 128] = jnp.where(
                lane_group + 8.0 * g == adapter_cols, rank_cols8, 0.0
            ).astype(jnp.bfloat16)
        up = up_base + contract_last(exp_ref[...], aout[...])
        gate = g_ref[...]
        h_ref[...] = (jax.nn.silu(gate) * up).astype(jnp.bfloat16)

        def down(j):
            block = pl.ds(pl.multiple_of(chip(j) * 2 * C, 2 * C), 2 * C)
            part[s, :, block] = jnp.dot(
                h_ref[...], dw[:, block], preferred_element_type=jnp.float32
            ).astype(jnp.bfloat16)
            r1_copy(s, j).start()

        def pair(j):
            r1_copy(s, j).wait_recv()
            where = col(chip(j))
            pair_sum[s, :, where] = (
                part[s, :, col(2 * chip(j) + c)].astype(jnp.float32)
                + pair_in[s, :, where].astype(jnp.float32)
            ).astype(jnp.bfloat16)

        down(3)
        down(1)
        pair(3)
        d_copy(s, 1).start()
        d_copy(s, 2).start()
        down(2)
        pair(1)
        n_copy(s, 1, 0).start()
        down(0)
        pair(2)
        n_copy(s, 2, 1).start()
        pair(0)

        @pl.when(s > 0)
        def _():
            quad_finish(s - 1)

        @pl.when(s > 1)
        def _():
            e_copy(s - 1).start()

        return carry

    lax.fori_loop(0, 4, step, 0)
    quad_middle(3)
    quad_finish(3)
    e_copy(3).start()

    mixed = w_cols[:, 0:1] * e_buf[0].astype(jnp.float32)
    for s in range(1, 4):
        e_copy(s).wait_recv()
        mixed = mixed + w_cols[:, s : s + 1] * back[s].astype(jnp.float32)
    out_ref[...] = mixed.astype(jnp.bfloat16)

    for s in range(1, 4):
        z_copy(s).wait_send()
        e_copy(s).wait_send()

    def drain(s, carry):
        for j in (1, 2):
            xy_copy(s, j).wait_send()
            dg_copy(s, j).wait_send()
        for j in range(4):
            sib_copy(s, j).wait_send()
            r1_copy(s, j).wait_send()
        for j in (1, 2):
            d_copy(s, j).wait_send()
            for h in range(2):
                n_copy(s, j, h).wait_send()
        for d in range(1, 8):
            rk_copy(s, d).wait_send()
        return carry

    lax.fori_loop(0, 4, drain, 0)


def fused(
    tokens,
    expert_route,
    route_gate,
    request_lengths,
    request_adapter,
    request_order,
    gate_weight,
    up_weight,
    down_weight,
    adapter_in,
    adapter_out,
):
    T, C = tokens.shape
    D = gate_weight.shape[2]
    F = gate_weight.shape[1]
    A = adapter_in.shape[1]
    bf16 = jnp.bfloat16
    dma = pltpu.SemaphoreType.DMA
    vmem = pl.BlockSpec(memory_space=pltpu.VMEM)
    smem = pl.BlockSpec(memory_space=pltpu.SMEM)
    hbm = pl.BlockSpec(memory_space=pl.ANY)
    return pl.pallas_call(
        kernel,
        out_shape=jax.ShapeDtypeStruct((T, C), bf16),
        in_specs=[smem, smem, smem, hbm, vmem, vmem, hbm, hbm, hbm, hbm, hbm],
        out_specs=vmem,
        scratch_shapes=[
            pltpu.VMEM((F, D), bf16),
            pltpu.VMEM((F, D), bf16),
            pltpu.VMEM((F, D), bf16),
            pltpu.VMEM((A, D), bf16),
            pltpu.VMEM((F, ADAPTERS * RANK), bf16),
            pltpu.VMEM((4, T, D), bf16),
            pltpu.VMEM((4, T, D), bf16),
            pltpu.VMEM((4, T, 4 * C), bf16),
            pltpu.VMEM((4, T, 4 * C), bf16),
            pltpu.VMEM((4, 4, T, C), bf16),
            pltpu.VMEM((4, T, C), bf16),
            pltpu.VMEM((4, T, C), bf16),
            pltpu.VMEM((4, 8, RANK, T), bf16),
            pltpu.VMEM((4, 1, T), jnp.int32),
            pltpu.VMEM((T, F), jnp.float32),
            pltpu.VMEM((T, ADAPTERS * RANK), bf16),
            pltpu.VMEM((T, F), bf16),
            pltpu.VMEM((T, 128), jnp.float32),
            dma((5,)),
            dma,
            dma((4,)),
            dma((4,)),
            dma((4, 4)),
            dma((4, 4)),
            dma((4, 4)),
            dma((4, 4)),
            dma((4, 4)),
            dma((4, 4)),
            dma((4, 8)),
            dma((4, 8)),
            dma((4, 4)),
            dma((4, 4)),
            dma((4, 4)),
            dma((4, 4)),
            dma((4, 4)),
            dma((4, 4)),
            dma((4,)),
            dma((4,)),
        ],
        compiler_params=pltpu.CompilerParams(
            collective_id=0, has_side_effects=True, vmem_limit_bytes=60 * 1024 * 1024
        ),
        cost_estimate=pl.CostEstimate(
            flops=8 * T * (3 * F * D + A * D + F * ADAPTERS * RANK),
            bytes_accessed=2 * (3 * F * D + A * D + F * ADAPTERS * RANK),
            transcendentals=4 * T * F,
        ),
    )(
        request_lengths,
        request_adapter,
        request_order,
        tokens,
        expert_route.T,
        route_gate.T,
        gate_weight,
        up_weight,
        down_weight,
        adapter_in,
        adapter_out,
    )


def solution(mesh):
    in_specs = (
        P("expert", "mp"),
        P("expert", None),
        P("expert", None),
        P(),
        P(),
        P(),
        P("expert", "mp", None),
        P("expert", "mp", None),
        P("expert", "mp", None),
        P("expert", "mp", None),
        P("expert", "mp", None),
    )
    out_specs = P("expert", "mp")
    small = mesh.shape["expert"] == 4 and mesh.shape["mp"] == 8
    return jax.shard_map(
        fused if small else plain,
        mesh=mesh, in_specs=in_specs, out_specs=out_specs, check_vma=False,
    )
```

```python
import functools

import jax
import jax.numpy as jnp
from jax import lax
from jax.experimental import pallas as pl
from jax.experimental.pallas import tpu as pltpu
from jax.sharding import PartitionSpec as P

RANK = 16
ADAPTERS = 64
MESH = pl.DeviceIdType.MESH


def contract_last(left, right):
    return lax.dot_general(
        left, right, (((1,), (1,)), ((), ())), preferred_element_type=jnp.float32
    )


def token_adapters(request_lengths, request_adapter, request_order, token_count):
    request_ids = jnp.arange(request_lengths.shape[0], dtype=jnp.int32)
    chosen = (request_order[:, None] == request_ids[None, :]).astype(jnp.int32)
    packed_lengths = jnp.sum(chosen * request_lengths[None, :], axis=1, dtype=jnp.int32)
    packed_adapters = jnp.sum(chosen * request_adapter[None, :], axis=1, dtype=jnp.int32)
    boundary = jnp.cumsum(packed_lengths, dtype=jnp.int32)
    positions = jnp.arange(token_count, dtype=jnp.int32)
    packed_index = jnp.sum(
        (boundary[None, :] <= positions[:, None]).astype(jnp.int32), axis=1, dtype=jnp.int32
    )
    matches = (packed_index[:, None] == request_ids[None, :]).astype(jnp.int32)
    return jnp.sum(matches * packed_adapters[None, :], axis=1, dtype=jnp.int32)


def plain(
    tokens,
    expert_route,
    route_gate,
    request_lengths,
    request_adapter,
    request_order,
    gate_weight,
    up_weight,
    down_weight,
    adapter_in,
    adapter_out,
):
    groups = lax.axis_size("expert")
    tok_rows, cols = tokens.shape
    own_rows = lax.all_gather(tokens, "expert", axis=0, tiled=True)
    rows = lax.all_gather(own_rows, "mp", axis=1, tiled=True)
    row_count = rows.shape[0]
    adapter_of = token_adapters(request_lengths, request_adapter, request_order, row_count)
    rank_w = adapter_in[0]
    rank_cols = contract_last(rows, rank_w)
    per_device = rank_w.shape[0] // RANK
    local_adapter = adapter_of - lax.axis_index("mp") * per_device
    local_pick = (
        local_adapter[:, None] == jnp.arange(per_device, dtype=jnp.int32)[None, :]
    ).astype(jnp.float32)
    rank_part = jnp.sum(
        rank_cols.reshape(row_count, per_device, RANK) * local_pick[:, :, None], axis=1
    )
    rank = lax.psum(rank_part.astype(jnp.bfloat16), "mp")
    gate_pre = contract_last(rows, gate_weight[0])
    up_base = contract_last(rows, up_weight[0])
    chosen = (adapter_of[:, None] == jnp.arange(ADAPTERS, dtype=jnp.int32)[None, :]).astype(
        jnp.bfloat16
    )
    expanded = (rank[:, None, :] * chosen[:, :, None]).reshape(row_count, ADAPTERS * RANK)
    up = up_base + contract_last(expanded, adapter_out[0])
    hidden = (jax.nn.silu(gate_pre) * up).astype(jnp.bfloat16)
    partial = jnp.dot(hidden, down_weight[0], preferred_element_type=jnp.float32)
    mine = lax.psum_scatter(
        partial.astype(jnp.bfloat16), "mp", scatter_dimension=1, tiled=True
    )
    back = lax.all_to_all(
        mine.reshape(groups, tok_rows, cols), "expert", split_axis=0, concat_axis=0, tiled=True
    )
    expert_ids = jnp.arange(groups, dtype=jnp.int32)
    weights = jnp.sum(
        jnp.where(expert_route[:, :, None] == expert_ids, route_gate[:, :, None], 0.0), axis=1
    )
    mixed = jnp.sum(weights.T[:, :, None] * back.astype(jnp.float32), axis=0)
    return mixed.astype(jnp.bfloat16)


def xor4(a, b):
    return (a + b) % 2 + 2 * ((a // 2 + b // 2) % 2)


def mask_of(s):
    return s // 2 + 2 * (((s + 1) // 2) % 2)


def kernel(
    len_ref,
    req_adapter_ref,
    order_ref,
    tok_ref,
    route_ref,
    weigh_ref,
    gw_hbm,
    uw_hbm,
    dw_hbm,
    ain_hbm,
    aout_hbm,
    out_ref,
    gw,
    uw,
    dw,
    ain,
    aout,
    x_buf,
    part,
    pair_in,
    pair_sum,
    quad_in,
    e_buf,
    back,
    rk_buf,
    adp,
    g_ref,
    u_ref,
    exp_ref,
    h_ref,
    w_cols,
    w_sem,
    loc_sem,
    z_send,
    z_recv,
    xy_send,
    xy_recv,
    dg_send,
    dg_recv,
    sib_send,
    sib_recv,
    rk_send,
    rk_recv,
    r1_send,
    r1_recv,
    r2_send,
    r2_recv,
    n_send,
    n_recv,
    e_send,
    e_recv,
):
    T, C = tok_ref.shape
    H = T // 2
    z = lax.axis_index("expert")
    m = lax.axis_index("mp")
    q = m // 2
    c = m % 2
    sibling = (z, 2 * q + 1 - c)

    def chip(j):
        return xor4(q, j)

    def col(index):
        return pl.ds(pl.multiple_of(index * C, C), C)

    def remote(src, dst, send, recv, target):
        return pltpu.make_async_remote_copy(
            src_ref=src, dst_ref=dst, send_sem=send, recv_sem=recv,
            device_id=target, device_id_type=MESH,
        )

    def z_copy(s):
        return remote(
            x_buf.at[0, :, col(m)], x_buf.at[s, :, col(m)],
            z_send.at[s], z_recv.at[s], (xor4(z, mask_of(s)), m),
        )

    def xy_copy(s, j):
        ref = x_buf.at[s, :, col(m)]
        return remote(ref, ref, xy_send.at[s, j], xy_recv.at[s, j], (z, 2 * chip(j) + c))

    def dg_copy(s, j):
        ref = x_buf.at[s, pl.ds(H * (j - 1), H), col(2 * chip(j) + c)]
        return remote(
            ref, ref, dg_send.at[s, j], dg_recv.at[s, j], (z, 2 * chip(3 - j) + c)
        )

    def sib_copy(s, j):
        ref = x_buf.at[s, :, col(2 * chip(j) + c)]
        return remote(ref, ref, sib_send.at[s, j], sib_recv.at[s, j], sibling)

    def rk_copy(s, d):
        return remote(
            rk_buf.at[s, 0], rk_buf.at[s, d],
            rk_send.at[s, d], rk_recv.at[s, d], (z, (m + d) % 8),
        )

    def r1_copy(s, j):
        return remote(
            part.at[s, :, col(2 * chip(j) + 1 - c)], pair_in.at[s, :, col(chip(j))],
            r1_send.at[s, j], r1_recv.at[s, j], sibling,
        )

    def half(h):
        return pl.ds(H * h, H)

    def d_copy(s, j):
        return remote(
            pair_sum.at[s, half(j - 1), col(chip(3))], quad_in.at[s, 3, half(j - 1)],
            r2_send.at[s, j], r2_recv.at[s, j], (z, 2 * chip(j) + c),
        )

    def n_copy(s, j, h):
        i = 2 * (j - 1) + h
        return remote(
            pair_sum.at[s, half(h), col(chip(j))], quad_in.at[s, j, half(h)],
            n_send.at[s, i], n_recv.at[s, i], (z, 2 * chip(j) + c),
        )

    def e_copy(s):
        return remote(e_buf.at[s], back.at[s], e_send.at[s], e_recv.at[s], (xor4(z, mask_of(s)), m))

    first = pltpu.make_async_copy(tok_ref, x_buf.at[0, :, col(m)], loc_sem)
    first.start()
    weights = [
        pltpu.make_async_copy(src.at[0], dst, w_sem.at[i])
        for i, (src, dst) in enumerate(
            ((ain_hbm, ain), (gw_hbm, gw), (uw_hbm, uw), (aout_hbm, aout), (dw_hbm, dw))
        )
    ]
    for copy in weights:
        copy.start()

    barrier = pltpu.get_barrier_semaphore()
    for s in range(1, 4):
        pl.semaphore_signal(barrier, inc=1, device_id=(xor4(z, mask_of(s)), m), device_id_type=MESH)
    for d in range(1, 8):
        pl.semaphore_signal(barrier, inc=1, device_id=(z, (m + d) % 8), device_id_type=MESH)
    pl.semaphore_wait(barrier, 10)

    first.wait()

    def begin(s):
        for j in (1, 2):
            xy_copy(s, j).start()
        sib_copy(s, 0).start()

    def forward(s):
        for j in (1, 2):
            xy_copy(s, j).wait_recv()
            dg_copy(s, j).start()
            sib_copy(s, j).start()

    def late(s):
        for j in (1, 2):
            dg_copy(s, j).wait_recv()
        sib_copy(s, 3).start()

    def finish(s):
        for j in range(4):
            sib_copy(s, j).wait_recv()

    z_copy(1).start()
    begin(0)

    start = jnp.int32(0)
    starts, ids = [], []
    for j in range(len_ref.shape[0]):
        request = order_ref[j]
        starts.append(start)
        ids.append(req_adapter_ref[request])
        start = start + len_ref[request]
    for s in range(4):
        position = xor4(z, mask_of(s)) * T + lax.broadcasted_iota(jnp.int32, (1, T), 1)
        value = jnp.zeros((1, T), jnp.int32)
        for at, adapter in zip(starts, ids):
            value = jnp.where(position >= at, adapter, value)
        adp[s] = value

    hits = [
        jnp.sum(
            jnp.where(route_ref[...] == xor4(z, mask_of(s)), weigh_ref[...], 0.0),
            axis=0, keepdims=True,
        )
        for s in range(4)
    ]
    w_cols[...] = jnp.concatenate(hits + [jnp.zeros((124, T), jnp.float32)], axis=0).T

    forward(0)
    z_copy(2).start()
    z_copy(3).start()
    z_copy(1).wait_recv()
    begin(1)
    late(0)
    for copy in weights:
        copy.wait()

    def quad_middle(s):
        for j in (1, 2):
            h = j - 1
            d_copy(s, j).wait_recv()
            where = col(chip(3 - j))
            pair_sum[s, half(h), where] = (
                pair_sum[s, half(h), where].astype(jnp.float32)
                + quad_in[s, 3, half(h)].astype(jnp.float32)
            ).astype(jnp.bfloat16)
            n_copy(s, 3 - j, h).start()

    def quad_finish(s):
        for j in (1, 2):
            for h in range(2):
                n_copy(s, j, h).wait_recv()
        e_buf[s] = (
            pair_sum[s, :, col(q)].astype(jnp.float32)
            + quad_in[s, 1].astype(jnp.float32)
            + quad_in[s, 2].astype(jnp.float32)
        ).astype(jnp.bfloat16)

    per_device = ain.shape[0] // RANK

    def send_rank(s):
        rank_cols = contract_last(ain[...], x_buf[s])
        group = lax.broadcasted_iota(jnp.int32, rank_cols.shape, 0) // RANK + per_device * m
        picked = jnp.where(group == adp[s], rank_cols, 0.0)
        total = picked[0:RANK]
        for g in range(1, per_device):
            total = total + picked[g * RANK : (g + 1) * RANK]
        rk_buf[s, 0] = total.astype(jnp.bfloat16)
        for d in range(1, 8):
            rk_copy(s, d).start()

    finish(0)
    send_rank(0)
    g_ref[...] = contract_last(x_buf[0], gw[...])
    forward(1)
    u_ref[...] = contract_last(x_buf[0], uw[...])

    def step(s, carry):
        @pl.when(s < 2)
        def _():
            z_copy(s + 2).wait_recv()
            begin(s + 2)

        @pl.when(s < 3)
        def _():
            late(s + 1)

        adapter_row = adp[s]
        for d in range(1, 8):
            rk_copy(s, d).wait_recv()
        rank = rk_buf[s, 0].astype(jnp.float32)
        for d in range(1, 8):
            rank = rank + rk_buf[s, d].astype(jnp.float32)
        rank_cols8 = jnp.concatenate([rank] * 8, axis=0).T
        adapter_cols = jnp.broadcast_to(adapter_row.astype(jnp.float32), (128, T)).T
        lane_group = (lax.broadcasted_iota(jnp.int32, (T, 128), 1) // RANK).astype(jnp.float32)
        for g in range(ADAPTERS // 8):
            exp_ref[:, g * 128 : (g + 1) * 128] = jnp.where(
                lane_group + 8.0 * g == adapter_cols, rank_cols8, 0.0
            ).astype(jnp.bfloat16)
        up = u_ref[...] + contract_last(exp_ref[...], aout[...])
        gate = g_ref[...]
        h_ref[...] = (jax.nn.silu(gate) * up).astype(jnp.bfloat16)

        @pl.when(s < 3)
        def _():
            finish(s + 1)
            send_rank(s + 1)

        def down(j):
            block = pl.ds(pl.multiple_of(chip(j) * 2 * C, 2 * C), 2 * C)
            part[s, :, block] = jnp.dot(
                h_ref[...], dw[:, block], preferred_element_type=jnp.float32
            ).astype(jnp.bfloat16)
            r1_copy(s, j).start()

        def pair(j):
            r1_copy(s, j).wait_recv()
            where = col(chip(j))
            pair_sum[s, :, where] = (
                part[s, :, col(2 * chip(j) + c)].astype(jnp.float32)
                + pair_in[s, :, where].astype(jnp.float32)
            ).astype(jnp.bfloat16)

        down(3)
        down(1)
        pair(3)
        d_copy(s, 1).start()
        d_copy(s, 2).start()
        down(2)
        pair(1)
        n_copy(s, 1, 0).start()
        down(0)
        pair(2)
        n_copy(s, 2, 1).start()
        pair(0)

        @pl.when(s > 0)
        def _():
            quad_finish(s - 1)

        @pl.when(s > 1)
        def _():
            e_copy(s - 1).start()

        @pl.when(s < 2)
        def _():
            forward(s + 2)

        @pl.when(s < 3)
        def _():
            g_ref[...] = contract_last(x_buf[s + 1], gw[...])

        quad_middle(s)

        @pl.when(s < 3)
        def _():
            u_ref[...] = contract_last(x_buf[s + 1], uw[...])

        return carry

    lax.fori_loop(0, 4, step, 0)
    quad_finish(3)
    e_copy(3).start()

    mixed = w_cols[:, 0:1] * e_buf[0].astype(jnp.float32)
    for s in range(1, 4):
        e_copy(s).wait_recv()
        mixed = mixed + w_cols[:, s : s + 1] * back[s].astype(jnp.float32)
    out_ref[...] = mixed.astype(jnp.bfloat16)

    for s in range(1, 4):
        z_copy(s).wait_send()
        e_copy(s).wait_send()

    def drain(s, carry):
        for j in (1, 2):
            xy_copy(s, j).wait_send()
            dg_copy(s, j).wait_send()
        for j in range(4):
            sib_copy(s, j).wait_send()
            r1_copy(s, j).wait_send()
        for j in (1, 2):
            d_copy(s, j).wait_send()
            for h in range(2):
                n_copy(s, j, h).wait_send()
        for d in range(1, 8):
            rk_copy(s, d).wait_send()
        return carry

    lax.fori_loop(0, 4, drain, 0)


def fused(
    tokens,
    expert_route,
    route_gate,
    request_lengths,
    request_adapter,
    request_order,
    gate_weight,
    up_weight,
    down_weight,
    adapter_in,
    adapter_out,
):
    T, C = tokens.shape
    D = gate_weight.shape[2]
    F = gate_weight.shape[1]
    A = adapter_in.shape[1]
    bf16 = jnp.bfloat16
    dma = pltpu.SemaphoreType.DMA
    vmem = pl.BlockSpec(memory_space=pltpu.VMEM)
    smem = pl.BlockSpec(memory_space=pltpu.SMEM)
    hbm = pl.BlockSpec(memory_space=pl.ANY)
    return pl.pallas_call(
        kernel,
        out_shape=jax.ShapeDtypeStruct((T, C), bf16),
        in_specs=[smem, smem, smem, hbm, vmem, vmem, hbm, hbm, hbm, hbm, hbm],
        out_specs=vmem,
        scratch_shapes=[
            pltpu.VMEM((F, D), bf16),
            pltpu.VMEM((F, D), bf16),
            pltpu.VMEM((F, D), bf16),
            pltpu.VMEM((A, D), bf16),
            pltpu.VMEM((F, ADAPTERS * RANK), bf16),
            pltpu.VMEM((4, T, D), bf16),
            pltpu.VMEM((4, T, D), bf16),
            pltpu.VMEM((4, T, 4 * C), bf16),
            pltpu.VMEM((4, T, 4 * C), bf16),
            pltpu.VMEM((4, 4, T, C), bf16),
            pltpu.VMEM((4, T, C), bf16),
            pltpu.VMEM((4, T, C), bf16),
            pltpu.VMEM((4, 8, RANK, T), bf16),
            pltpu.VMEM((4, 1, T), jnp.int32),
            pltpu.VMEM((T, F), jnp.float32),
            pltpu.VMEM((T, F), jnp.float32),
            pltpu.VMEM((T, ADAPTERS * RANK), bf16),
            pltpu.VMEM((T, F), bf16),
            pltpu.VMEM((T, 128), jnp.float32),
            dma((5,)),
            dma,
            dma((4,)),
            dma((4,)),
            dma((4, 4)),
            dma((4, 4)),
            dma((4, 4)),
            dma((4, 4)),
            dma((4, 4)),
            dma((4, 4)),
            dma((4, 8)),
            dma((4, 8)),
            dma((4, 4)),
            dma((4, 4)),
            dma((4, 4)),
            dma((4, 4)),
            dma((4, 4)),
            dma((4, 4)),
            dma((4,)),
            dma((4,)),
        ],
        compiler_params=pltpu.CompilerParams(
            collective_id=0, has_side_effects=True, vmem_limit_bytes=60 * 1024 * 1024
        ),
        cost_estimate=pl.CostEstimate(
            flops=8 * T * (3 * F * D + A * D + F * ADAPTERS * RANK),
            bytes_accessed=2 * (3 * F * D + A * D + F * ADAPTERS * RANK),
            transcendentals=4 * T * F,
        ),
    )(
        request_lengths,
        request_adapter,
        request_order,
        tokens,
        expert_route.T,
        route_gate.T,
        gate_weight,
        up_weight,
        down_weight,
        adapter_in,
        adapter_out,
    )


def solution(mesh):
    in_specs = (
        P("expert", "mp"),
        P("expert", None),
        P("expert", None),
        P(),
        P(),
        P(),
        P("expert", "mp", None),
        P("expert", "mp", None),
        P("expert", "mp", None),
        P("expert", "mp", None),
        P("expert", "mp", None),
    )
    out_specs = P("expert", "mp")
    small = mesh.shape["expert"] == 4 and mesh.shape["mp"] == 8
    return jax.shard_map(
        fused if small else plain,
        mesh=mesh, in_specs=in_specs, out_specs=out_specs, check_vma=False,
    )
```

```python
import functools

import jax
import jax.numpy as jnp
from jax import lax
from jax.experimental import pallas as pl
from jax.experimental.pallas import tpu as pltpu
from jax.sharding import PartitionSpec as P

RANK = 16
ADAPTERS = 64
MESH = pl.DeviceIdType.MESH


def contract_last(left, right):
    return lax.dot_general(
        left, right, (((1,), (1,)), ((), ())), preferred_element_type=jnp.float32
    )


def token_adapters(request_lengths, request_adapter, request_order, token_count):
    request_ids = jnp.arange(request_lengths.shape[0], dtype=jnp.int32)
    chosen = (request_order[:, None] == request_ids[None, :]).astype(jnp.int32)
    packed_lengths = jnp.sum(chosen * request_lengths[None, :], axis=1, dtype=jnp.int32)
    packed_adapters = jnp.sum(chosen * request_adapter[None, :], axis=1, dtype=jnp.int32)
    boundary = jnp.cumsum(packed_lengths, dtype=jnp.int32)
    positions = jnp.arange(token_count, dtype=jnp.int32)
    packed_index = jnp.sum(
        (boundary[None, :] <= positions[:, None]).astype(jnp.int32), axis=1, dtype=jnp.int32
    )
    matches = (packed_index[:, None] == request_ids[None, :]).astype(jnp.int32)
    return jnp.sum(matches * packed_adapters[None, :], axis=1, dtype=jnp.int32)


def plain(
    tokens,
    expert_route,
    route_gate,
    request_lengths,
    request_adapter,
    request_order,
    gate_weight,
    up_weight,
    down_weight,
    adapter_in,
    adapter_out,
):
    groups = lax.axis_size("expert")
    tok_rows, cols = tokens.shape
    own_rows = lax.all_gather(tokens, "expert", axis=0, tiled=True)
    rows = lax.all_gather(own_rows, "mp", axis=1, tiled=True)
    row_count = rows.shape[0]
    adapter_of = token_adapters(request_lengths, request_adapter, request_order, row_count)
    rank_w = adapter_in[0]
    rank_cols = contract_last(rows, rank_w)
    per_device = rank_w.shape[0] // RANK
    local_adapter = adapter_of - lax.axis_index("mp") * per_device
    local_pick = (
        local_adapter[:, None] == jnp.arange(per_device, dtype=jnp.int32)[None, :]
    ).astype(jnp.float32)
    rank_part = jnp.sum(
        rank_cols.reshape(row_count, per_device, RANK) * local_pick[:, :, None], axis=1
    )
    rank = lax.psum(rank_part.astype(jnp.bfloat16), "mp")
    gate_pre = contract_last(rows, gate_weight[0])
    up_base = contract_last(rows, up_weight[0])
    chosen = (adapter_of[:, None] == jnp.arange(ADAPTERS, dtype=jnp.int32)[None, :]).astype(
        jnp.bfloat16
    )
    expanded = (rank[:, None, :] * chosen[:, :, None]).reshape(row_count, ADAPTERS * RANK)
    up = up_base + contract_last(expanded, adapter_out[0])
    hidden = (jax.nn.silu(gate_pre) * up).astype(jnp.bfloat16)
    partial = jnp.dot(hidden, down_weight[0], preferred_element_type=jnp.float32)
    mine = lax.psum_scatter(
        partial.astype(jnp.bfloat16), "mp", scatter_dimension=1, tiled=True
    )
    back = lax.all_to_all(
        mine.reshape(groups, tok_rows, cols), "expert", split_axis=0, concat_axis=0, tiled=True
    )
    expert_ids = jnp.arange(groups, dtype=jnp.int32)
    weights = jnp.sum(
        jnp.where(expert_route[:, :, None] == expert_ids, route_gate[:, :, None], 0.0), axis=1
    )
    mixed = jnp.sum(weights.T[:, :, None] * back.astype(jnp.float32), axis=0)
    return mixed.astype(jnp.bfloat16)


def xor4(a, b):
    return (a + b) % 2 + 2 * ((a // 2 + b // 2) % 2)


def mask_of(s):
    return s // 2 + 2 * (((s + 1) // 2) % 2)


def kernel(
    len_ref,
    req_adapter_ref,
    order_ref,
    tok_ref,
    route_ref,
    weigh_ref,
    gw_hbm,
    uw_hbm,
    dw_hbm,
    ain_hbm,
    aout_hbm,
    out_ref,
    gw,
    uw,
    dw,
    ain,
    aout,
    x_buf,
    part,
    pair_in,
    pair_sum,
    quad_in,
    e_buf,
    back,
    rk_buf,
    adp,
    g_ref,
    u_ref,
    exp_ref,
    h_ref,
    w_cols,
    w_sem,
    loc_sem,
    z_send,
    z_recv,
    xy_send,
    xy_recv,
    dg_send,
    dg_recv,
    sib_send,
    sib_recv,
    rk_send,
    rk_recv,
    r1_send,
    r1_recv,
    r2_send,
    r2_recv,
    n_send,
    n_recv,
    e_send,
    e_recv,
):
    T, C = tok_ref.shape
    H = T // 2
    z = lax.axis_index("expert")
    m = lax.axis_index("mp")
    q = m // 2
    c = m % 2
    sibling = (z, 2 * q + 1 - c)

    def chip(j):
        return xor4(q, j)

    def col(index):
        return pl.ds(pl.multiple_of(index * C, C), C)

    def remote(src, dst, send, recv, target):
        return pltpu.make_async_remote_copy(
            src_ref=src, dst_ref=dst, send_sem=send, recv_sem=recv,
            device_id=target, device_id_type=MESH,
        )

    def z_copy(s):
        return remote(
            x_buf.at[0, :, col(m)], x_buf.at[s, :, col(m)],
            z_send.at[s], z_recv.at[s], (xor4(z, mask_of(s)), m),
        )

    def xy_copy(s, j):
        ref = x_buf.at[s, :, col(m)]
        return remote(ref, ref, xy_send.at[s, j], xy_recv.at[s, j], (z, 2 * chip(j) + c))

    def dg_copy(s, j):
        ref = x_buf.at[s, pl.ds(H * (j - 1), H), col(2 * chip(j) + c)]
        return remote(
            ref, ref, dg_send.at[s, j], dg_recv.at[s, j], (z, 2 * chip(3 - j) + c)
        )

    def sib_copy(s, j):
        ref = x_buf.at[s, :, col(2 * chip(j) + c)]
        return remote(ref, ref, sib_send.at[s, j], sib_recv.at[s, j], sibling)

    def rk_copy(s, d):
        return remote(
            rk_buf.at[s, 0], rk_buf.at[s, d],
            rk_send.at[s, d], rk_recv.at[s, d], (z, (m + d) % 8),
        )

    def r1_copy(s, j):
        return remote(
            part.at[s, :, col(2 * chip(j) + 1 - c)], pair_in.at[s, :, col(chip(j))],
            r1_send.at[s, j], r1_recv.at[s, j], sibling,
        )

    def half(h):
        return pl.ds(H * h, H)

    def d_copy(s, j):
        return remote(
            pair_sum.at[s, half(j - 1), col(chip(3))], quad_in.at[s, 3, half(j - 1)],
            r2_send.at[s, j], r2_recv.at[s, j], (z, 2 * chip(j) + c),
        )

    def n_copy(s, j, h):
        i = 2 * (j - 1) + h
        return remote(
            pair_sum.at[s, half(h), col(chip(j))], quad_in.at[s, j, half(h)],
            n_send.at[s, i], n_recv.at[s, i], (z, 2 * chip(j) + c),
        )

    def e_copy(s):
        return remote(e_buf.at[s], back.at[s], e_send.at[s], e_recv.at[s], (xor4(z, mask_of(s)), m))

    first = pltpu.make_async_copy(tok_ref, x_buf.at[0, :, col(m)], loc_sem)
    first.start()
    weights = [
        pltpu.make_async_copy(src.at[0], dst, w_sem.at[i])
        for i, (src, dst) in enumerate(
            ((ain_hbm, ain), (gw_hbm, gw), (uw_hbm, uw), (aout_hbm, aout), (dw_hbm, dw))
        )
    ]
    for copy in weights:
        copy.start()

    barrier = pltpu.get_barrier_semaphore()
    for s in range(1, 4):
        pl.semaphore_signal(barrier, inc=1, device_id=(xor4(z, mask_of(s)), m), device_id_type=MESH)
    for d in range(1, 8):
        pl.semaphore_signal(barrier, inc=1, device_id=(z, (m + d) % 8), device_id_type=MESH)
    pl.semaphore_wait(barrier, 10)

    first.wait()

    def begin(s):
        for j in (1, 2):
            xy_copy(s, j).start()
        sib_copy(s, 0).start()

    def forward(s):
        for j in (1, 2):
            xy_copy(s, j).wait_recv()
            dg_copy(s, j).start()
            sib_copy(s, j).start()

    def late(s):
        for j in (1, 2):
            dg_copy(s, j).wait_recv()
        sib_copy(s, 3).start()

    def finish(s):
        for j in range(4):
            sib_copy(s, j).wait_recv()

    z_copy(1).start()
    begin(0)

    start = jnp.int32(0)
    starts, ids = [], []
    for j in range(len_ref.shape[0]):
        request = order_ref[j]
        starts.append(start)
        ids.append(req_adapter_ref[request])
        start = start + len_ref[request]
    for s in range(4):
        position = xor4(z, mask_of(s)) * T + lax.broadcasted_iota(jnp.int32, (1, T), 1)
        value = jnp.zeros((1, T), jnp.int32)
        for at, adapter in zip(starts, ids):
            value = jnp.where(position >= at, adapter, value)
        adp[s] = value

    hits = [
        jnp.sum(
            jnp.where(route_ref[...] == xor4(z, mask_of(s)), weigh_ref[...], 0.0),
            axis=0, keepdims=True,
        )
        for s in range(4)
    ]
    w_cols[...] = jnp.concatenate(hits + [jnp.zeros((124, T), jnp.float32)], axis=0).T

    forward(0)
    z_copy(2).start()
    z_copy(3).start()
    z_copy(1).wait_recv()
    begin(1)
    late(0)
    for copy in weights:
        copy.wait()

    def quad_middle(s):
        for j in (1, 2):
            h = j - 1
            d_copy(s, j).wait_recv()
            where = col(chip(3 - j))
            pair_sum[s, half(h), where] = (
                pair_sum[s, half(h), where].astype(jnp.float32)
                + quad_in[s, 3, half(h)].astype(jnp.float32)
            ).astype(jnp.bfloat16)
            n_copy(s, 3 - j, h).start()

    def quad_finish(s):
        for j in (1, 2):
            for h in range(2):
                n_copy(s, j, h).wait_recv()
        e_buf[s] = (
            pair_sum[s, :, col(q)].astype(jnp.float32)
            + quad_in[s, 1].astype(jnp.float32)
            + quad_in[s, 2].astype(jnp.float32)
        ).astype(jnp.bfloat16)

    per_device = ain.shape[0] // RANK

    def send_rank(s):
        rank_cols = contract_last(ain[...], x_buf[s])
        group = lax.broadcasted_iota(jnp.int32, rank_cols.shape, 0) // RANK + per_device * m
        picked = jnp.where(group == adp[s], rank_cols, 0.0)
        total = picked[0:RANK]
        for g in range(1, per_device):
            total = total + picked[g * RANK : (g + 1) * RANK]
        rk_buf[s, 0] = total.astype(jnp.bfloat16)
        for d in range(1, 8):
            rk_copy(s, d).start()

    finish(0)
    send_rank(0)
    g_ref[...] = contract_last(x_buf[0], gw[...])
    forward(1)
    u_ref[...] = contract_last(x_buf[0], uw[...])

    def step(s, carry):
        @pl.when(s < 2)
        def _():
            z_copy(s + 2).wait_recv()
            begin(s + 2)

        @pl.when(s < 3)
        def _():
            late(s + 1)

        adapter_row = adp[s]
        for d in range(1, 8):
            rk_copy(s, d).wait_recv()
        rank = rk_buf[s, 0].astype(jnp.float32)
        for d in range(1, 8):
            rank = rank + rk_buf[s, d].astype(jnp.float32)
        rank_cols8 = jnp.concatenate([rank] * 8, axis=0).T
        adapter_cols = jnp.broadcast_to(adapter_row.astype(jnp.float32), (128, T)).T
        lane_group = (lax.broadcasted_iota(jnp.int32, (T, 128), 1) // RANK).astype(jnp.float32)
        for g in range(ADAPTERS // 8):
            exp_ref[:, g * 128 : (g + 1) * 128] = jnp.where(
                lane_group + 8.0 * g == adapter_cols, rank_cols8, 0.0
            ).astype(jnp.bfloat16)
        up = u_ref[...] + contract_last(exp_ref[...], aout[...])
        gate = g_ref[...]
        h_ref[...] = (jax.nn.silu(gate) * up).astype(jnp.bfloat16)

        @pl.when(s < 3)
        def _():
            finish(s + 1)
            send_rank(s + 1)

        def down(j):
            block = pl.ds(pl.multiple_of(chip(j) * 2 * C, 2 * C), 2 * C)
            part[s, :, block] = jnp.dot(
                h_ref[...], dw[:, block], preferred_element_type=jnp.float32
            ).astype(jnp.bfloat16)
            r1_copy(s, j).start()

        def pair(j):
            r1_copy(s, j).wait_recv()
            where = col(chip(j))
            pair_sum[s, :, where] = (
                part[s, :, col(2 * chip(j) + c)].astype(jnp.float32)
                + pair_in[s, :, where].astype(jnp.float32)
            ).astype(jnp.bfloat16)

        down(3)
        down(1)
        pair(3)
        d_copy(s, 1).start()
        d_copy(s, 2).start()

        @pl.when(s > 0)
        def _():
            quad_finish(s - 1)

        @pl.when(s > 1)
        def _():
            e_copy(s - 1).start()

        down(2)
        pair(1)
        n_copy(s, 1, 0).start()
        down(0)
        pair(2)
        n_copy(s, 2, 1).start()
        pair(0)

        @pl.when(s < 2)
        def _():
            forward(s + 2)

        @pl.when(s < 3)
        def _():
            g_ref[...] = contract_last(x_buf[s + 1], gw[...])

        quad_middle(s)

        @pl.when(s < 3)
        def _():
            u_ref[...] = contract_last(x_buf[s + 1], uw[...])

        return carry

    lax.fori_loop(0, 4, step, 0)
    quad_finish(3)
    e_copy(3).start()

    mixed = w_cols[:, 0:1] * e_buf[0].astype(jnp.float32)
    for s in range(1, 4):
        e_copy(s).wait_recv()
        mixed = mixed + w_cols[:, s : s + 1] * back[s].astype(jnp.float32)
    out_ref[...] = mixed.astype(jnp.bfloat16)

    for s in range(1, 4):
        z_copy(s).wait_send()
        e_copy(s).wait_send()

    def drain(s, carry):
        for j in (1, 2):
            xy_copy(s, j).wait_send()
            dg_copy(s, j).wait_send()
        for j in range(4):
            sib_copy(s, j).wait_send()
            r1_copy(s, j).wait_send()
        for j in (1, 2):
            d_copy(s, j).wait_send()
            for h in range(2):
                n_copy(s, j, h).wait_send()
        for d in range(1, 8):
            rk_copy(s, d).wait_send()
        return carry

    lax.fori_loop(0, 4, drain, 0)


def fused(
    tokens,
    expert_route,
    route_gate,
    request_lengths,
    request_adapter,
    request_order,
    gate_weight,
    up_weight,
    down_weight,
    adapter_in,
    adapter_out,
):
    T, C = tokens.shape
    D = gate_weight.shape[2]
    F = gate_weight.shape[1]
    A = adapter_in.shape[1]
    bf16 = jnp.bfloat16
    dma = pltpu.SemaphoreType.DMA
    vmem = pl.BlockSpec(memory_space=pltpu.VMEM)
    smem = pl.BlockSpec(memory_space=pltpu.SMEM)
    hbm = pl.BlockSpec(memory_space=pl.ANY)
    return pl.pallas_call(
        kernel,
        out_shape=jax.ShapeDtypeStruct((T, C), bf16),
        in_specs=[smem, smem, smem, hbm, vmem, vmem, hbm, hbm, hbm, hbm, hbm],
        out_specs=vmem,
        scratch_shapes=[
            pltpu.VMEM((F, D), bf16),
            pltpu.VMEM((F, D), bf16),
            pltpu.VMEM((F, D), bf16),
            pltpu.VMEM((A, D), bf16),
            pltpu.VMEM((F, ADAPTERS * RANK), bf16),
            pltpu.VMEM((4, T, D), bf16),
            pltpu.VMEM((4, T, D), bf16),
            pltpu.VMEM((4, T, 4 * C), bf16),
            pltpu.VMEM((4, T, 4 * C), bf16),
            pltpu.VMEM((4, 4, T, C), bf16),
            pltpu.VMEM((4, T, C), bf16),
            pltpu.VMEM((4, T, C), bf16),
            pltpu.VMEM((4, 8, RANK, T), bf16),
            pltpu.VMEM((4, 1, T), jnp.int32),
            pltpu.VMEM((T, F), jnp.float32),
            pltpu.VMEM((T, F), jnp.float32),
            pltpu.VMEM((T, ADAPTERS * RANK), bf16),
            pltpu.VMEM((T, F), bf16),
            pltpu.VMEM((T, 128), jnp.float32),
            dma((5,)),
            dma,
            dma((4,)),
            dma((4,)),
            dma((4, 4)),
            dma((4, 4)),
            dma((4, 4)),
            dma((4, 4)),
            dma((4, 4)),
            dma((4, 4)),
            dma((4, 8)),
            dma((4, 8)),
            dma((4, 4)),
            dma((4, 4)),
            dma((4, 4)),
            dma((4, 4)),
            dma((4, 4)),
            dma((4, 4)),
            dma((4,)),
            dma((4,)),
        ],
        compiler_params=pltpu.CompilerParams(
            collective_id=0, has_side_effects=True, vmem_limit_bytes=60 * 1024 * 1024
        ),
        cost_estimate=pl.CostEstimate(
            flops=8 * T * (3 * F * D + A * D + F * ADAPTERS * RANK),
            bytes_accessed=2 * (3 * F * D + A * D + F * ADAPTERS * RANK),
            transcendentals=4 * T * F,
        ),
    )(
        request_lengths,
        request_adapter,
        request_order,
        tokens,
        expert_route.T,
        route_gate.T,
        gate_weight,
        up_weight,
        down_weight,
        adapter_in,
        adapter_out,
    )


def solution(mesh):
    in_specs = (
        P("expert", "mp"),
        P("expert", None),
        P("expert", None),
        P(),
        P(),
        P(),
        P("expert", "mp", None),
        P("expert", "mp", None),
        P("expert", "mp", None),
        P("expert", "mp", None),
        P("expert", "mp", None),
    )
    out_specs = P("expert", "mp")
    small = mesh.shape["expert"] == 4 and mesh.shape["mp"] == 8
    return jax.shard_map(
        fused if small else plain,
        mesh=mesh, in_specs=in_specs, out_specs=out_specs, check_vma=False,
    )
```
